128 devices in a mesh: rows: 64 (over y, z_hi, x, core), frames: 2 (over z_lo).
Axes of the slice: x: 4, y: 4, z: 4 (z_hi: 2, z_lo: 2; z = z_hi * 2 + z_lo), core: 2. Of those that a mesh axis runs over, the one named last changes fastest.
Arguments:
- video: bfloat16 [8, 768, 512, 128], P('frames', 'rows'), may hold values from -6 to 6
- spatial_kernel: bfloat16 [3, 3, 128, 128], replicated, may hold values from -0.1875 to 0.1875
- spatial_bias: float32 [128], replicated, may hold values from -3 to 3
- temporal_kernel: bfloat16 [3, 128, 128], replicated, may hold values from -0.3125 to 0.3125
- temporal_bias: float32 [128], replicated, may hold values from -3 to 3
Outputs:
- doubled: bfloat16 [16, 768, 512, 128], P('frames', None, 'rows')
The draws below stay inside these ranges and needn't reach their ends.
All inputs are finite; a program needn't handle non-finite values.
Results may differ from the reference program's by a relative error of at most 0.0052.
Values may be sent and summed in bfloat16 or wider, within the bound.
A program may use at most 192 MiB of HBM per device.

```python
import jax
import jax.numpy as jnp
from jax import lax

C = 128
FRAMES = 8
W = 512
H = 768


def level_of(key, shape, cuts, least, top_value):
    def one(axis_at, blocks):
        draws = jax.random.uniform(jax.random.fold_in(jax.random.fold_in(key, 6), axis_at), (blocks,), jnp.float32, least / len(cuts), top_value / len(cuts))
        return jnp.repeat(jnp.exp(draws), shape[axis_at] // blocks).reshape((-1,) + (1,) * (len(shape) - axis_at - 1))

    factor_of = one(*cuts[0])
    for cut in cuts[1:]:
        factor_of = factor_of * one(*cut)
    return factor_of


def bell_draw(rng, dims, width, limit, pieces=(), kind=jnp.bfloat16):
    drawn = width * jax.random.normal(rng, dims, jnp.float32)
    if pieces:
        drawn = drawn * level_of(rng, dims, pieces, -0.22, 0.18)
    return jnp.clip(drawn, -limit, limit).astype(kind)


def setup_inputs(seed: int = 0) -> dict:
    key_of = jax.random.split(jax.random.key(seed), 6)
    return {
        "video": bell_draw(key_of[0], (FRAMES, H, W, C), 1.0, 6.0, ((0, 2), (1, 64))),
        "spatial_kernel": bell_draw(key_of[1], (3, 3, C, C), (9 * C) ** -0.5, 0.1875),
        "spatial_bias": bell_draw(key_of[2], (C,), 0.5, 3.0, (), jnp.float32),
        "temporal_kernel": bell_draw(key_of[3], (3, C, C), (3 * C) ** -0.5, 0.3125),
        "temporal_bias": bell_draw(key_of[4], (C,), 0.5, 3.0, (), jnp.float32),
    }


def conv_frame(frame, spatial_kernel, spatial_bias):
    result = lax.conv_general_dilated(frame[None], spatial_kernel, (1, 1), ((1, 1), (1, 1)), dimension_numbers=("NHWC", "HWIO", "NHWC"), preferred_element_type=jnp.float32)[0]
    return (result + spatial_bias).astype(jnp.bfloat16)


def reference(video, spatial_kernel, spatial_bias, temporal_kernel, temporal_bias):
    spatial = lax.map(lambda frame: conv_frame(frame, spatial_kernel, spatial_bias), video)
    widened = spatial.astype(jnp.float32)
    middles = (widened[:-1] + widened[1:]) * 0.5
    middles = jnp.concatenate([middles, widened[-1:]], axis=0)
    upsampled = jnp.stack([widened, middles], axis=1).reshape((2 * FRAMES,) + spatial.shape[1:]).astype(jnp.bfloat16)
    padded = jnp.pad(upsampled, ((1, 1), (0, 0), (0, 0), (0, 0)))

    def one_frame(index):
        window = lax.dynamic_slice_in_dim(padded, index, 3, 0).astype(jnp.float32)
        total = window[1] + temporal_bias
        for shift in range(3):
            total = total + jnp.einsum("hwc,cd->hwd", window[shift], temporal_kernel[shift].astype(jnp.float32))
        return total.astype(jnp.bfloat16)

    return lax.map(one_frame, jnp.arange(2 * FRAMES, dtype=jnp.int32))
```

```python
import jax
import jax.numpy as jnp
from jax import lax
from jax.experimental import pallas as pl
from jax.experimental.pallas import tpu as pltpu
from jax.sharding import PartitionSpec as P

MESH = pl.DeviceIdType.MESH
C = 128
F = 4
R = 12
W = 512
N = 64
COLS = W // N
BLOCK = R * COLS
TILE = 768


def partner(row, step):
    dx = step % 4
    dy = (step // 4 + step) % 4
    dw = (step // 16 + step) % 4
    y = (row // 16 + dy) % 4
    z = (row // 8 + dw // 2) % 2
    x = (row // 2 + dx) % 4
    core = (row + dw) % 2
    return ((y * 2 + z) * 4 + x) * 2 + core


def spatial_kernel_body(
    video, taps, bias, received, rows, left, right, outgoing, weights,
    load_sem, rim_send, rim_recv, send_sem, recv_sem, own_sem,
):
    me = lax.axis_index("rows")
    side = lax.axis_index("frames")
    barrier = pltpu.get_barrier_semaphore()

    @pl.loop(0, N)
    def _(step):
        peer = partner(me, step)

        @pl.when(step > 0)
        def _():
            pl.semaphore_signal(barrier, inc=1, device_id=(peer, side), device_id_type=MESH)

        pl.semaphore_signal(barrier, inc=1, device_id=(peer, 1 - side), device_id_type=MESH)

    def frame_at(step):
        return (step + 3 * (1 - side)) % F

    def load(frame):
        return pltpu.make_async_copy(video.at[frame], rows.at[frame, pl.ds(1, R)], load_sem.at[frame])

    for step in range(F):
        load(frame_at(step)).start()

    for b in range(3):
        for j in range(4):
            for o in range(2):
                a = j - o
                block = taps[a, b] if 0 <= a < 3 else jnp.zeros((C, C), jnp.bfloat16)
                weights[pl.ds((b * 4 + j) * C, C), pl.ds(o * C, C)] = block

    pl.semaphore_wait(barrier, 2 * N - 1)

    def rim_copies(frame):
        up = pltpu.make_async_remote_copy(
            src_ref=video.at[frame, 0], dst_ref=rows.at[frame, R + 1],
            send_sem=rim_send.at[frame, 0], recv_sem=rim_recv.at[frame, 0],
            device_id=((me + N - 1) % N, side), device_id_type=MESH,
        )
        down = pltpu.make_async_remote_copy(
            src_ref=video.at[frame, R - 1], dst_ref=rows.at[frame, 0],
            send_sem=rim_send.at[frame, 1], recv_sem=rim_recv.at[frame, 1],
            device_id=((me + 1) % N, side), device_id_type=MESH,
        )
        return up, down

    for step in range(F):
        for copy in rim_copies(frame_at(step)):
            copy.start()

    column = lax.broadcasted_iota(jnp.int32, (W, C), 0)

    @pl.loop(0, F)
    def _(step):
        frame = frame_at(step)
        load(frame).wait()
        for copy in rim_copies(frame):
            copy.wait()

        @pl.when(me == 0)
        def _():
            rows[frame, 0] = jnp.zeros((W, C), jnp.bfloat16)

        @pl.when(me == N - 1)
        def _():
            rows[frame, R + 1] = jnp.zeros((W, C), jnp.bfloat16)

        @pl.loop(0, R + 2)
        def _(i):
            row = rows[frame, i].astype(jnp.float32)
            left[i] = jnp.where(column == 0, 0.0, pltpu.roll(row, 1, 0)).astype(jnp.bfloat16)
            right[i] = jnp.where(column == W - 1, 0.0, pltpu.roll(row, W - 1, 0)).astype(jnp.bfloat16)

        @pl.loop(0, R // 2)
        def _(pair):
            first = 2 * pair
            pieces = (
                [left[first + j] for j in range(4)]
                + [rows[frame, first + j] for j in range(4)]
                + [right[first + j] for j in range(4)]
            )
            total = jnp.dot(
                jnp.concatenate(pieces, axis=1), weights[...], preferred_element_type=jnp.float32
            )
            upper = (total[:, :C] + bias[...]).reshape(N, COLS, C)
            lower = (total[:, C:] + bias[...]).reshape(N, COLS, C)
            both = jnp.concatenate([upper, lower], axis=1).astype(jnp.bfloat16)
            outgoing[frame, :, pl.ds(pl.multiple_of(pair * 2 * COLS, 2 * COLS), 2 * COLS), :] = both

        pltpu.make_async_copy(
            outgoing.at[frame, me], received.at[frame, me], own_sem.at[frame]
        ).start()

        @pl.loop(0, N)
        def _(index):
            peer = partner(me, index)

            @pl.when(index > 0)
            def _():
                pltpu.make_async_remote_copy(
                    src_ref=outgoing.at[frame, peer], dst_ref=received.at[frame, me],
                    send_sem=send_sem.at[frame], recv_sem=recv_sem.at[frame],
                    device_id=(peer, side), device_id_type=MESH,
                ).start()

            @pl.when(step == 0)
            def _():
                pltpu.make_async_remote_copy(
                    src_ref=outgoing.at[frame, peer], dst_ref=received.at[F, me],
                    send_sem=send_sem.at[F], recv_sem=recv_sem.at[F],
                    device_id=(peer, 1 - side), device_id_type=MESH,
                ).start()

    def whole(slot, count, sem):
        part = received.at[slot, pl.ds(0, count)]
        return pltpu.make_async_copy(part, part, sem.at[slot])

    for frame in range(F):
        whole(frame, N - 1, send_sem).wait()
        whole(frame, N - 1, recv_sem).wait()
        pltpu.make_async_copy(
            outgoing.at[frame, me], received.at[frame, me], own_sem.at[frame]
        ).wait()
    whole(F, N, send_sem).wait()
    whole(F, N, recv_sem).wait()


def spatial_exchange(video, taps, bias):
    return pl.pallas_call(
        spatial_kernel_body,
        out_shape=jax.ShapeDtypeStruct((F + 1, N, BLOCK, C), jnp.bfloat16),
        in_specs=[
            pl.BlockSpec(memory_space=pl.ANY),
            pl.BlockSpec(memory_space=pltpu.VMEM),
            pl.BlockSpec(memory_space=pltpu.VMEM),
        ],
        out_specs=pl.BlockSpec(memory_space=pl.ANY),
        scratch_shapes=[
            pltpu.VMEM((F, R + 2, W, C), jnp.bfloat16),
            pltpu.VMEM((R + 2, W, C), jnp.bfloat16),
            pltpu.VMEM((R + 2, W, C), jnp.bfloat16),
            pltpu.VMEM((F, N, BLOCK, C), jnp.bfloat16),
            pltpu.VMEM((12 * C, 2 * C), jnp.bfloat16),
            pltpu.SemaphoreType.DMA((F,)),
            pltpu.SemaphoreType.DMA((F, 2)),
            pltpu.SemaphoreType.DMA((F, 2)),
            pltpu.SemaphoreType.DMA((F + 1,)),
            pltpu.SemaphoreType.DMA((F + 1,)),
            pltpu.SemaphoreType.DMA((F,)),
        ],
        compiler_params=pltpu.CompilerParams(
            collective_id=0, has_side_effects=True, vmem_limit_bytes=48 * 2**20
        ),
        cost_estimate=pl.CostEstimate(
            flops=2 * 9 * C * C * F * R * W, bytes_accessed=9 * R * W * C * 2, transcendentals=0
        ),
        name="spatial_exchange",
    )(video, taps, bias)


def temporal_kernel_body(frames, taps, bias, doubled, weights):
    side = lax.axis_index("frames")

    @pl.when(pl.program_id(0) == 0)
    def _():
        for j in range(4):
            for o in range(2):
                d = j - o
                block = taps[d] if 0 <= d < 3 else jnp.zeros((C, C), jnp.bfloat16)
                weights[pl.ds(j * C, C), pl.ds(o * C, C)] = block

    own = [frames[k].astype(jnp.float32) for k in range(F)]
    halo = frames[F].astype(jnp.float32)
    first_side = side == 0
    zero = jnp.zeros((TILE, C), jnp.float32)
    before = jnp.where(first_side, zero, (halo + own[0]) * 0.5).astype(jnp.bfloat16)
    after = jnp.where(first_side, halo, zero).astype(jnp.bfloat16)
    beyond = jnp.where(first_side, halo, own[F - 1])
    for k in range(F):
        middle = ((own[k] + (own[k + 1] if k + 1 < F else beyond)) * 0.5).astype(jnp.bfloat16)
        following = frames[k + 1] if k + 1 < F else after
        window = jnp.concatenate([before, frames[k], middle, following], axis=1)
        total = jnp.dot(window, weights[...], preferred_element_type=jnp.float32)
        doubled[2 * k] = (total[:, :C] + (own[k] + bias[...])).astype(jnp.bfloat16)
        doubled[2 * k + 1] = (
            total[:, C:] + (middle.astype(jnp.float32) + bias[...])
        ).astype(jnp.bfloat16)
        before = middle


def temporal(frames, taps, bias):
    count = N * BLOCK
    return pl.pallas_call(
        temporal_kernel_body,
        out_shape=jax.ShapeDtypeStruct((2 * F, count, C), jnp.bfloat16),
        grid=(count // TILE,),
        in_specs=[
            pl.BlockSpec((F + 1, TILE, C), lambda i: (0, i, 0)),
            pl.BlockSpec((3, C, C), lambda i: (0, 0, 0)),
            pl.BlockSpec((1, C), lambda i: (0, 0)),
        ],
        out_specs=pl.BlockSpec((2 * F, TILE, C), lambda i: (0, i, 0)),
        scratch_shapes=[pltpu.VMEM((4 * C, 2 * C), jnp.bfloat16)],
        compiler_params=pltpu.CompilerParams(vmem_limit_bytes=48 * 2**20),
        cost_estimate=pl.CostEstimate(
            flops=2 * 3 * C * C * 2 * F * count, bytes_accessed=13 * count * C * 2, transcendentals=0
        ),
        name="temporal",
    )(frames, taps, bias)


def per_device(video, spatial_kernel, spatial_bias, temporal_kernel, temporal_bias):
    received = spatial_exchange(video, spatial_kernel, spatial_bias.reshape(1, C))
    frames = received.reshape(F + 1, N * BLOCK, C)
    doubled = temporal(frames, temporal_kernel, temporal_bias.reshape(1, C))
    return doubled.reshape(2 * F, N * R, COLS, C)


def solution(mesh):
    placed = (P("frames", "rows", None, None), P(), P(), P(), P())
    return jax.shard_map(
        per_device,
        mesh=mesh,
        in_specs=placed,
        out_specs=P("frames", None, "rows", None),
        check_vma=False,
    )
```

```python
import jax
import jax.numpy as jnp
from jax import lax
from jax.experimental import pallas as pl
from jax.experimental.pallas import tpu as pltpu
from jax.sharding import PartitionSpec as P

MESH = pl.DeviceIdType.MESH
C = 128
F = 4
R = 12
W = 512
N = 64
COLS = W // N
BLOCK = R * COLS
COUNT = N * BLOCK
GROUP = 8
TILE = GROUP * BLOCK
BF16 = jnp.bfloat16
F32 = jnp.float32


def partner(row, step):
    mixed = (37 * step + 10 * step * step) % N
    y = (row // 16 + mixed // 16) % 4
    z = (row // 8 + mixed) % 2
    x = (row // 2 + mixed // 4) % 4
    core = (row + mixed // 2) % 2
    return ((y * 2 + z) * 4 + x) * 2 + core


def spread_taps(taps, weights):
    for j in range(4):
        for o in range(2):
            d = j - o
            block = taps[d] if 0 <= d < 3 else jnp.zeros((C, C), BF16)
            weights[pl.ds(j * C, C), pl.ds(o * C, C)] = block


def two_frames(before, frame, middle, following, weights, bias):
    window = jnp.concatenate([before, frame, middle, following], axis=1)
    total = jnp.dot(window, weights[...], preferred_element_type=F32)
    even = total[:, :C] + (frame.astype(F32) + bias)
    odd = total[:, C:] + (middle.astype(F32) + bias)
    return even.astype(BF16), odd.astype(BF16)


def exchange_body(
    video, spatial_taps, spatial_bias, temporal_taps, temporal_bias,
    received, early,
    rows, left, right, outgoing, weights, time_weights, taps, time_taps, bias, time_bias,
    load_sem, small_sem, rim_send, rim_recv, send_sem, recv_sem, own_sem,
):
    me = lax.axis_index("rows")
    side = lax.axis_index("frames")
    barrier = pltpu.get_barrier_semaphore()

    def frame_at(step):
        return step * (2 * side - 1) + (F - 1) * (1 - side)

    def load(frame):
        return pltpu.make_async_copy(video.at[frame], rows.at[frame, pl.ds(1, R)], load_sem.at[frame])

    load(frame_at(0)).start()
    small = [
        pltpu.make_async_copy(source, target, small_sem.at[k])
        for k, (source, target) in enumerate(
            [(spatial_taps, taps), (spatial_bias, bias), (temporal_taps, time_taps), (temporal_bias, time_bias)]
        )
    ]
    for copy in small:
        copy.start()

    @pl.loop(1, N, unroll=9)
    def _(step):
        peer = lax.rem(me + step, N)
        pl.semaphore_signal(barrier, inc=1, device_id=(peer, side), device_id_type=MESH)
        pl.semaphore_signal(barrier, inc=1, device_id=(peer, 1 - side), device_id_type=MESH)

    pl.semaphore_signal(barrier, inc=1, device_id=(me, 1 - side), device_id_type=MESH)

    for step in range(1, F):
        load(frame_at(step)).start()
    for copy in small:
        copy.wait()
    for b in range(3):
        for j in range(4):
            for o in range(2):
                a = j - o
                block = taps[a, b] if 0 <= a < 3 else jnp.zeros((C, C), BF16)
                weights[pl.ds((b * 4 + j) * C, C), pl.ds(o * C, C)] = block
    spread_taps(time_taps, time_weights)

    def rim_copies(frame):
        up = pltpu.make_async_remote_copy(
            src_ref=video.at[frame, 0], dst_ref=rows.at[frame, R + 1],
            send_sem=rim_send.at[frame, 0], recv_sem=rim_recv.at[frame, 0],
            device_id=((me + N - 1) % N, side), device_id_type=MESH,
        )
        down = pltpu.make_async_remote_copy(
            src_ref=video.at[frame, R - 1], dst_ref=rows.at[frame, 0],
            send_sem=rim_send.at[frame, 1], recv_sem=rim_recv.at[frame, 1],
            device_id=((me + 1) % N, side), device_id_type=MESH,
        )
        return up, down

    def wait_rims(frame):
        for copy in rim_copies(frame):
            copy.wait()

        @pl.when(me == 0)
        def _():
            rows[frame, 0] = jnp.zeros((W, C), BF16)

        @pl.when(me == N - 1)
        def _():
            rows[frame, R + 1] = jnp.zeros((W, C), BF16)

    column = lax.broadcasted_iota(jnp.int32, (W, C), 0)

    def shift(frame, i):
        row = rows[frame, i].astype(F32)
        left[i] = jnp.where(column == 0, 0.0, pltpu.roll(row, 1, 0)).astype(BF16)
        right[i] = jnp.where(column == W - 1, 0.0, pltpu.roll(row, W - 1, 0)).astype(BF16)

    def convolve(frame, pair):
        first = 2 * pair
        pieces = (
            [left[first + j] for j in range(4)]
            + [rows[frame, first + j] for j in range(4)]
            + [right[first + j] for j in range(4)]
        )
        total = jnp.dot(jnp.concatenate(pieces, axis=1), weights[...], preferred_element_type=F32)
        upper = (total[:, :C] + bias[...]).reshape(N, COLS, C)
        lower = (total[:, C:] + bias[...]).reshape(N, COLS, C)
        both = jnp.concatenate([upper, lower], axis=1).astype(BF16)
        outgoing[frame, :, pl.ds(pl.multiple_of(pair * 2 * COLS, 2 * COLS), 2 * COLS), :] = both

    def inner(frame):
        load(frame).wait()
        pl.loop(1, R + 1)(lambda i: shift(frame, i))
        pl.loop(1, R // 2 - 1)(lambda pair: convolve(frame, pair))

    def outer(frame):
        wait_rims(frame)
        pl.loop(0, 2)(lambda k: shift(frame, k * (R + 1)))
        pl.loop(0, 2)(lambda k: convolve(frame, k * (R // 2 - 1)))

    def own(frame):
        return pltpu.make_async_copy(outgoing.at[frame, me], received.at[frame, me], own_sem.at[frame])

    def send(frame, slot, peer, where):
        pltpu.make_async_remote_copy(
            src_ref=outgoing.at[frame, peer], dst_ref=received.at[slot, me],
            send_sem=send_sem.at[slot], recv_sem=recv_sem.at[slot],
            device_id=(peer, where), device_id_type=MESH,
        ).start()

    head = frame_at(0)
    inner(head)
    pl.semaphore_wait(barrier, 2 * N - 1)
    for step in range(F):
        for copy in rim_copies(frame_at(step)):
            copy.start()
    outer(head)
    send(head, F, me, 1 - side)

    @pl.loop(1, N)
    def _(index):
        peer = partner(me, index)
        send(head, head, peer, side)
        send(head, F, peer, 1 - side)

    own(head).start()

    @pl.loop(1, F)
    def _(step):
        frame = frame_at(step)
        inner(frame)
        outer(frame)

        @pl.loop(1, N)
        def _(index):
            send(frame, frame, partner(me, index), side)

        own(frame).start()

    def whole(slot, count, sem):
        part = received.at[slot, pl.ds(0, count)]
        return pltpu.make_async_copy(part, part, sem.at[slot])

    whole(F, N, recv_sem).wait()
    for step in range(F - 1):
        whole(frame_at(step), N - 1, recv_sem).wait()
        own(frame_at(step)).wait()

    slots = [1 + 3 * side, 2 - 2 * side, 3 - 2 * side, 4 - 2 * side]

    @pl.loop(0, N // GROUP)
    def _(index):
        blocks = pl.ds(pl.multiple_of(index * GROUP, GROUP), GROUP)
        out = pl.ds(pl.multiple_of(index * TILE, TILE), TILE)
        seen = [received[slot, blocks].reshape(TILE, C) for slot in slots]
        half = jnp.asarray(0.5, BF16)
        middles = [(seen[k] + seen[k + 1]) * half for k in range(3)]
        for k in range(2):
            even, odd = two_frames(
                middles[k], seen[k + 1], middles[k + 1], seen[k + 2], time_weights, time_bias[...]
            )
            early[2 * k, out] = even
            early[2 * k + 1, out] = odd

    last = frame_at(F - 1)
    for slot in range(F):
        whole(slot, N - 1, send_sem).wait()
    whole(F, N, send_sem).wait()
    whole(last, N - 1, recv_sem).wait()
    own(last).wait()


def exchange(video, spatial_taps, spatial_bias, temporal_taps, temporal_bias):
    return pl.pallas_call(
        exchange_body,
        out_shape=(
            pltpu.VMEM((F + 1, N, BLOCK, C), BF16),
            pltpu.VMEM((F, COUNT, C), BF16),
        ),
        in_specs=[pl.BlockSpec(memory_space=pltpu.HBM)] * 5,
        out_specs=[pl.BlockSpec(memory_space=pltpu.VMEM)] * 2,
        scratch_shapes=[
            pltpu.VMEM((F, R + 2, W, C), BF16),
            pltpu.VMEM((R + 2, W, C), BF16),
            pltpu.VMEM((R + 2, W, C), BF16),
            pltpu.VMEM((F, N, BLOCK, C), BF16),
            pltpu.VMEM((12 * C, 2 * C), BF16),
            pltpu.VMEM((4 * C, 2 * C), BF16),
            pltpu.VMEM((3, 3, C, C), BF16),
            pltpu.VMEM((3, C, C), BF16),
            pltpu.VMEM((1, C), F32),
            pltpu.VMEM((1, C), F32),
            pltpu.SemaphoreType.DMA((F,)),
            pltpu.SemaphoreType.DMA((4,)),
            pltpu.SemaphoreType.DMA((F, 2)),
            pltpu.SemaphoreType.DMA((F, 2)),
            pltpu.SemaphoreType.DMA((F + 1,)),
            pltpu.SemaphoreType.DMA((F + 1,)),
            pltpu.SemaphoreType.DMA((F,)),
        ],
        compiler_params=pltpu.CompilerParams(
            collective_id=0, has_side_effects=True, vmem_limit_bytes=30 * 2**20
        ),
        cost_estimate=pl.CostEstimate(
            flops=2 * 9 * C * C * F * R * W + 3 * C * C * 2 * F * COUNT,
            bytes_accessed=F * R * W * C * 2,
            transcendentals=0,
        ),
        name="spatial_exchange",
    )(
        *(
            pltpu.with_memory_space_constraint(operand, pltpu.HBM)
            for operand in (video, spatial_taps, spatial_bias, temporal_taps, temporal_bias)
        )
    )


def late_body(received, early, taps, bias, doubled, weights, late, early_sem, late_sem):
    side = lax.axis_index("frames")
    copies = [
        pltpu.make_async_copy(early.at[k], doubled.at[F * (1 - side) + k], early_sem.at[k]) for k in range(F)
    ]
    for copy in copies:
        copy.start()
    spread_taps(taps, weights)
    zero, half = jnp.asarray(0.0, BF16), jnp.asarray(0.5, BF16)
    slots = [side, 2 * side, 1 + 2 * side, 2 + side]

    def store(index):
        out = pl.ds(pl.multiple_of(index * TILE, TILE), TILE)
        return pltpu.make_async_copy(
            late.at[:, out], doubled.at[pl.ds(F * side, F), out], late_sem.at[index]
        )

    @pl.loop(0, N // GROUP)
    def _(index):
        blocks = pl.ds(pl.multiple_of(index * GROUP, GROUP), GROUP)
        out = pl.ds(pl.multiple_of(index * TILE, TILE), TILE)
        seen = [received[slot, blocks].reshape(TILE, C) for slot in slots]
        middles = [(seen[k] + seen[k + 1]) * half for k in range(3)]
        middles[0] = jnp.where(side == 0, zero, middles[0])
        middles[2] = jnp.where(side == 0, middles[2], seen[2])
        seen[3] = jnp.where(side == 0, seen[3], zero)
        for k in range(2):
            even, odd = two_frames(
                middles[k], seen[k + 1], middles[k + 1], seen[k + 2], weights, bias[...]
            )
            late[2 * k, out] = even
            late[2 * k + 1, out] = odd
        store(index).start()

    pl.loop(0, N // GROUP)(lambda index: store(index).wait())
    for copy in copies:
        copy.wait()


def finish(received, early, taps, bias):
    return pl.pallas_call(
        late_body,
        out_shape=jax.ShapeDtypeStruct((2 * F, COUNT, C), BF16),
        in_specs=[pl.BlockSpec(memory_space=pltpu.VMEM)] * 4,
        out_specs=pl.BlockSpec(memory_space=pl.ANY),
        scratch_shapes=[
            pltpu.VMEM((4 * C, 2 * C), BF16),
            pltpu.VMEM((F, COUNT, C), BF16),
            pltpu.SemaphoreType.DMA((F,)),
            pltpu.SemaphoreType.DMA((N // GROUP,)),
        ],
        compiler_params=pltpu.CompilerParams(vmem_limit_bytes=16 * 2**20),
        cost_estimate=pl.CostEstimate(
            flops=3 * C * C * 2 * F * COUNT, bytes_accessed=8 * COUNT * C * 2, transcendentals=0
        ),
        name="late_frames",
    )(
        pltpu.with_memory_space_constraint(received, pltpu.VMEM),
        pltpu.with_memory_space_constraint(early, pltpu.VMEM),
        taps,
        bias,
    )


def per_device(video, spatial_kernel, spatial_bias, temporal_kernel, temporal_bias):
    time_bias = temporal_bias.reshape(1, C)
    received, early = exchange(
        video, spatial_kernel, spatial_bias.reshape(1, C), temporal_kernel, time_bias
    )
    doubled = finish(received, early, temporal_kernel, time_bias)
    return doubled.reshape(2 * F, N * R, COLS, C)


def solution(mesh):
    placed = (P("frames", "rows", None, None), P(), P(), P(), P())
    return jax.shard_map(
        per_device,
        mesh=mesh,
        in_specs=placed,
        out_specs=P("frames", None, "rows", None),
        check_vma=False,
    )
```

```python
import jax
import jax.numpy as jnp
from jax import lax
from jax.experimental import pallas as pl
from jax.experimental.pallas import tpu as pltpu
from jax.sharding import PartitionSpec as P

MESH = pl.DeviceIdType.MESH
C = 128
F = 4
R = 12
W = 512
N = 64
COLS = W // N
BLOCK = R * COLS
EDGE = 2 * COLS
COUNT = N * BLOCK
GROUP = 8
TILE = GROUP * BLOCK
BF16 = jnp.bfloat16
F32 = jnp.float32


def partner(row, step):
    mixed = (37 * step + 10 * step * step) % N
    y = (row // 16 + mixed // 16) % 4
    z = (row // 8 + mixed) % 2
    x = (row // 2 + mixed // 4) % 4
    core = (row + mixed // 2) % 2
    return ((y * 2 + z) * 4 + x) * 2 + core


def spread_taps(taps, weights):
    for j in range(4):
        for o in range(2):
            d = j - o
            block = taps[d] if 0 <= d < 3 else jnp.zeros((C, C), BF16)
            weights[pl.ds(j * C, C), pl.ds(o * C, C)] = block


def two_frames(before, frame, middle, following, weights, bias):
    window = jnp.concatenate([before, frame, middle, following], axis=1)
    total = jnp.dot(window, weights[...], preferred_element_type=F32)
    even = total[:, :C] + (frame.astype(F32) + bias)
    odd = total[:, C:] + (middle.astype(F32) + bias)
    return even.astype(BF16), odd.astype(BF16)


def exchange_body(
    video, spatial_taps, spatial_bias, temporal_taps, temporal_bias,
    received, early,
    rows, left, right, outgoing, weights, time_weights, taps, time_taps, bias, time_bias,
    load_sem, small_sem, rim_send, rim_recv, send_sem, recv_sem, own_sem,
):
    me = lax.axis_index("rows")
    side = lax.axis_index("frames")
    barrier = pltpu.get_barrier_semaphore()

    def frame_at(step):
        return step * (2 * side - 1) + (F - 1) * (1 - side)

    def load(frame):
        return pltpu.make_async_copy(video.at[frame], rows.at[frame, pl.ds(1, R)], load_sem.at[frame])

    load(frame_at(0)).start()
    small = [
        pltpu.make_async_copy(source, target, small_sem.at[k])
        for k, (source, target) in enumerate(
            [(spatial_taps, taps), (spatial_bias, bias), (temporal_taps, time_taps), (temporal_bias, time_bias)]
        )
    ]
    for copy in small:
        copy.start()

    @pl.loop(1, N, unroll=9)
    def _(step):
        peer = lax.rem(me + step, N)
        pl.semaphore_signal(barrier, inc=1, device_id=(peer, side), device_id_type=MESH)
        pl.semaphore_signal(barrier, inc=1, device_id=(peer, 1 - side), device_id_type=MESH)

    pl.semaphore_signal(barrier, inc=1, device_id=(me, 1 - side), device_id_type=MESH)

    for step in range(1, F):
        load(frame_at(step)).start()
    for copy in small:
        copy.wait()
    for b in range(3):
        for j in range(4):
            for o in range(2):
                a = j - o
                block = taps[a, b] if 0 <= a < 3 else jnp.zeros((C, C), BF16)
                weights[pl.ds((b * 4 + j) * C, C), pl.ds(o * C, C)] = block
    spread_taps(time_taps, time_weights)

    def rim_copies(frame):
        up = pltpu.make_async_remote_copy(
            src_ref=video.at[frame, 0], dst_ref=rows.at[frame, R + 1],
            send_sem=rim_send.at[frame, 0], recv_sem=rim_recv.at[frame, 0],
            device_id=((me + N - 1) % N, side), device_id_type=MESH,
        )
        down = pltpu.make_async_remote_copy(
            src_ref=video.at[frame, R - 1], dst_ref=rows.at[frame, 0],
            send_sem=rim_send.at[frame, 1], recv_sem=rim_recv.at[frame, 1],
            device_id=((me + 1) % N, side), device_id_type=MESH,
        )
        return up, down

    def wait_rims(frame):
        for copy in rim_copies(frame):
            copy.wait()

        @pl.when(me == 0)
        def _():
            rows[frame, 0] = jnp.zeros((W, C), BF16)

        @pl.when(me == N - 1)
        def _():
            rows[frame, R + 1] = jnp.zeros((W, C), BF16)

    column = lax.broadcasted_iota(jnp.int32, (W, C), 0)

    def shift(frame, i):
        row = rows[frame, i].astype(F32)
        left[i] = jnp.where(column == 0, 0.0, pltpu.roll(row, 1, 0)).astype(BF16)
        right[i] = jnp.where(column == W - 1, 0.0, pltpu.roll(row, W - 1, 0)).astype(BF16)

    def convolve(frame, pair):
        first = 2 * pair
        pieces = (
            [left[first + j] for j in range(4)]
            + [rows[frame, first + j] for j in range(4)]
            + [right[first + j] for j in range(4)]
        )
        total = jnp.dot(jnp.concatenate(pieces, axis=1), weights[...], preferred_element_type=F32)
        upper = (total[:, :C] + bias[...]).reshape(N, COLS, C)
        lower = (total[:, C:] + bias[...]).reshape(N, COLS, C)
        both = jnp.concatenate([upper, lower], axis=1).astype(BF16)
        outgoing[frame, :, pl.ds(pl.multiple_of(pair * 2 * COLS, 2 * COLS), 2 * COLS), :] = both

    def inner(frame):
        load(frame).wait()
        pl.loop(1, R + 1)(lambda i: shift(frame, i))
        pl.loop(1, R // 2 - 1)(lambda pair: convolve(frame, pair))

    def outer(frame):
        wait_rims(frame)
        pl.loop(0, 2)(lambda k: shift(frame, k * (R + 1)))
        pl.loop(0, 2)(lambda k: convolve(frame, k * (R // 2 - 1)))

    def own(frame):
        return pltpu.make_async_copy(outgoing.at[frame, me], received.at[frame, me], own_sem.at[frame])

    def send(frame, slot, peer, where, start=0, size=BLOCK):
        part = pl.ds(start, size)
        pltpu.make_async_remote_copy(
            src_ref=outgoing.at[frame, peer, part], dst_ref=received.at[slot, me, part],
            send_sem=send_sem.at[slot], recv_sem=recv_sem.at[slot],
            device_id=(peer, where), device_id_type=MESH,
        ).start()

    head = frame_at(0)
    inner(head)
    pl.semaphore_wait(barrier, 2 * N - 1)
    for copy in rim_copies(head):
        copy.start()

    @pl.loop(1, N)
    def _(index):
        send(head, head, partner(me, index), side, EDGE, BLOCK - 2 * EDGE)

    for step in range(1, F):
        for copy in rim_copies(frame_at(step)):
            copy.start()
    outer(head)
    send(head, F, me, 1 - side)

    @pl.loop(1, N)
    def _(index):
        peer = partner(me, index)
        send(head, F, peer, 1 - side)
        send(head, head, peer, side, 0, EDGE)
        send(head, head, peer, side, BLOCK - EDGE, EDGE)

    own(head).start()

    @pl.loop(1, F)
    def _(step):
        frame = frame_at(step)
        inner(frame)
        outer(frame)

        def in_order(early):
            @pl.loop(1, N)
            def _(index):
                peer = partner(me, index)
                near = ((peer // 2) % 4 == 0) | ((peer // 2) % 4 == 3)

                @pl.when(((step < F - 1) | near) if early else ((step == F - 1) & jnp.logical_not(near)))
                def _():
                    send(frame, frame, peer, side)

        in_order(True)
        in_order(False)
        own(frame).start()

    def whole(slot, count, sem):
        part = received.at[slot, pl.ds(0, count)]
        return pltpu.make_async_copy(part, part, sem.at[slot])

    whole(F, N, recv_sem).wait()
    for step in range(F - 1):
        whole(frame_at(step), N - 1, recv_sem).wait()
        own(frame_at(step)).wait()

    slots = [1 + 3 * side, 2 - 2 * side, 3 - 2 * side, 4 - 2 * side]

    @pl.loop(0, N // GROUP)
    def _(index):
        blocks = pl.ds(pl.multiple_of(index * GROUP, GROUP), GROUP)
        out = pl.ds(pl.multiple_of(index * TILE, TILE), TILE)
        seen = [received[slot, blocks].reshape(TILE, C) for slot in slots]
        half = jnp.asarray(0.5, BF16)
        middles = [(seen[k] + seen[k + 1]) * half for k in range(3)]
        for k in range(2):
            even, odd = two_frames(
                middles[k], seen[k + 1], middles[k + 1], seen[k + 2], time_weights, time_bias[...]
            )
            early[2 * k, out] = even
            early[2 * k + 1, out] = odd

    last = frame_at(F - 1)
    for slot in range(F):
        whole(slot, N - 1, send_sem).wait()
    whole(F, N, send_sem).wait()
    whole(last, N - 1, recv_sem).wait()
    own(last).wait()


def exchange(video, spatial_taps, spatial_bias, temporal_taps, temporal_bias):
    return pl.pallas_call(
        exchange_body,
        out_shape=(
            pltpu.VMEM((F + 1, N, BLOCK, C), BF16),
            pltpu.VMEM((F, COUNT, C), BF16),
        ),
        in_specs=[pl.BlockSpec(memory_space=pltpu.HBM)] * 5,
        out_specs=[pl.BlockSpec(memory_space=pltpu.VMEM)] * 2,
        scratch_shapes=[
            pltpu.VMEM((F, R + 2, W, C), BF16),
            pltpu.VMEM((R + 2, W, C), BF16),
            pltpu.VMEM((R + 2, W, C), BF16),
            pltpu.VMEM((F, N, BLOCK, C), BF16),
            pltpu.VMEM((12 * C, 2 * C), BF16),
            pltpu.VMEM((4 * C, 2 * C), BF16),
            pltpu.VMEM((3, 3, C, C), BF16),
            pltpu.VMEM((3, C, C), BF16),
            pltpu.VMEM((1, C), F32),
            pltpu.VMEM((1, C), F32),
            pltpu.SemaphoreType.DMA((F,)),
            pltpu.SemaphoreType.DMA((4,)),
            pltpu.SemaphoreType.DMA((F, 2)),
            pltpu.SemaphoreType.DMA((F, 2)),
            pltpu.SemaphoreType.DMA((F + 1,)),
            pltpu.SemaphoreType.DMA((F + 1,)),
            pltpu.SemaphoreType.DMA((F,)),
        ],
        compiler_params=pltpu.CompilerParams(
            collective_id=0, has_side_effects=True, vmem_limit_bytes=30 * 2**20
        ),
        cost_estimate=pl.CostEstimate(
            flops=2 * 9 * C * C * F * R * W + 3 * C * C * 2 * F * COUNT,
            bytes_accessed=F * R * W * C * 2,
            transcendentals=0,
        ),
        name="spatial_exchange",
    )(
        *(
            pltpu.with_memory_space_constraint(operand, pltpu.HBM)
            for operand in (video, spatial_taps, spatial_bias, temporal_taps, temporal_bias)
        )
    )


def late_body(received, early, taps, bias, doubled, weights, late, early_sem, late_sem):
    side = lax.axis_index("frames")
    copies = [
        pltpu.make_async_copy(early.at[k], doubled.at[F * (1 - side) + k], early_sem.at[k]) for k in range(F)
    ]
    for copy in copies:
        copy.start()
    spread_taps(taps, weights)
    zero, half = jnp.asarray(0.0, BF16), jnp.asarray(0.5, BF16)
    slots = [side, 2 * side, 1 + 2 * side, 2 + side]

    def store(index):
        out = pl.ds(pl.multiple_of(index * TILE, TILE), TILE)
        return pltpu.make_async_copy(
            late.at[:, out], doubled.at[pl.ds(F * side, F), out], late_sem.at[index]
        )

    @pl.loop(0, N // GROUP)
    def _(index):
        blocks = pl.ds(pl.multiple_of(index * GROUP, GROUP), GROUP)
        out = pl.ds(pl.multiple_of(index * TILE, TILE), TILE)
        seen = [received[slot, blocks].reshape(TILE, C) for slot in slots]
        middles = [(seen[k] + seen[k + 1]) * half for k in range(3)]
        middles[0] = jnp.where(side == 0, zero, middles[0])
        middles[2] = jnp.where(side == 0, middles[2], seen[2])
        seen[3] = jnp.where(side == 0, seen[3], zero)
        for k in range(2):
            even, odd = two_frames(
                middles[k], seen[k + 1], middles[k + 1], seen[k + 2], weights, bias[...]
            )
            late[2 * k, out] = even
            late[2 * k + 1, out] = odd
        store(index).start()

    pl.loop(0, N // GROUP)(lambda index: store(index).wait())
    for copy in copies:
        copy.wait()


def finish(received, early, taps, bias):
    return pl.pallas_call(
        late_body,
        out_shape=jax.ShapeDtypeStruct((2 * F, COUNT, C), BF16),
        in_specs=[pl.BlockSpec(memory_space=pltpu.VMEM)] * 4,
        out_specs=pl.BlockSpec(memory_space=pl.ANY),
        scratch_shapes=[
            pltpu.VMEM((4 * C, 2 * C), BF16),
            pltpu.VMEM((F, COUNT, C), BF16),
            pltpu.SemaphoreType.DMA((F,)),
            pltpu.SemaphoreType.DMA((N // GROUP,)),
        ],
        compiler_params=pltpu.CompilerParams(vmem_limit_bytes=16 * 2**20),
        cost_estimate=pl.CostEstimate(
            flops=3 * C * C * 2 * F * COUNT, bytes_accessed=8 * COUNT * C * 2, transcendentals=0
        ),
        name="late_frames",
    )(
        pltpu.with_memory_space_constraint(received, pltpu.VMEM),
        pltpu.with_memory_space_constraint(early, pltpu.VMEM),
        taps,
        bias,
    )


def per_device(video, spatial_kernel, spatial_bias, temporal_kernel, temporal_bias):
    time_bias = temporal_bias.reshape(1, C)
    received, early = exchange(
        video, spatial_kernel, spatial_bias.reshape(1, C), temporal_kernel, time_bias
    )
    doubled = finish(received, early, temporal_kernel, time_bias)
    return doubled.reshape(2 * F, N * R, COLS, C)


def solution(mesh):
    placed = (P("frames", "rows", None, None), P(), P(), P(), P())
    return jax.shard_map(
        per_device,
        mesh=mesh,
        in_specs=placed,
        out_specs=P("frames", None, "rows", None),
        check_vma=False,
    )
```

```python
import jax
import jax.numpy as jnp
from jax import lax
from jax.experimental import pallas as pl
from jax.experimental.pallas import tpu as pltpu
from jax.sharding import PartitionSpec as P

MESH = pl.DeviceIdType.MESH
C = 128
F = 4
R = 12
W = 512
N = 64
COLS = W // N
BLOCK = R * COLS
EDGE = 2 * COLS
COUNT = N * BLOCK
GROUP = 8
TILE = GROUP * BLOCK
BF16 = jnp.bfloat16
F32 = jnp.float32


def partner(row, step):
    mixed = (37 * step + 10 * step * step) % N
    y = (row // 16 + mixed // 16) % 4
    z = (row // 8 + mixed) % 2
    x = (row // 2 + mixed // 4) % 4
    core = (row + mixed // 2) % 2
    return ((y * 2 + z) * 4 + x) * 2 + core


def spread_taps(taps, weights):
    for j in range(4):
        for o in range(2):
            d = j - o
            block = taps[d] if 0 <= d < 3 else jnp.zeros((C, C), BF16)
            weights[pl.ds(j * C, C), pl.ds(o * C, C)] = block


def two_frames(before, frame, middle, following, weights, bias):
    window = jnp.concatenate([before, frame, middle, following], axis=1)
    total = jnp.dot(window, weights[...], preferred_element_type=F32)
    even = total[:, :C] + (frame.astype(F32) + bias)
    odd = total[:, C:] + (middle.astype(F32) + bias)
    return even.astype(BF16), odd.astype(BF16)


def exchange_body(
    video, spatial_taps, spatial_bias, temporal_taps, temporal_bias,
    received, early,
    rows, left, right, outgoing, weights, time_weights, taps, time_taps, bias, time_bias,
    load_sem, small_sem, rim_send, rim_recv, send_sem, recv_sem, own_sem,
):
    me = lax.axis_index("rows")
    side = lax.axis_index("frames")
    barrier = pltpu.get_barrier_semaphore()

    def frame_at(step):
        return step * (2 * side - 1) + (F - 1) * (1 - side)

    def load(frame):
        return pltpu.make_async_copy(video.at[frame], rows.at[frame, pl.ds(1, R)], load_sem.at[frame])

    load(frame_at(0)).start()
    small = [
        pltpu.make_async_copy(source, target, small_sem.at[k])
        for k, (source, target) in enumerate(
            [(spatial_taps, taps), (spatial_bias, bias), (temporal_taps, time_taps), (temporal_bias, time_bias)]
        )
    ]
    for copy in small:
        copy.start()

    @pl.loop(1, N, unroll=63)
    def _(step):
        peer = me + step - N * ((me + step) // N)
        pl.semaphore_signal(barrier, inc=1, device_id=(peer, side), device_id_type=MESH)
        pl.semaphore_signal(barrier, inc=1, device_id=(peer, 1 - side), device_id_type=MESH)

    pl.semaphore_signal(barrier, inc=1, device_id=(me, 1 - side), device_id_type=MESH)

    for step in range(1, F):
        load(frame_at(step)).start()
    for copy in small:
        copy.wait()
    for b in range(3):
        for j in range(4):
            for o in range(2):
                a = j - o
                block = taps[a, b] if 0 <= a < 3 else jnp.zeros((C, C), BF16)
                weights[pl.ds((b * 4 + j) * C, C), pl.ds(o * C, C)] = block
    spread_taps(time_taps, time_weights)

    def rim_copies(frame):
        up = pltpu.make_async_remote_copy(
            src_ref=video.at[frame, 0], dst_ref=rows.at[frame, R + 1],
            send_sem=rim_send.at[frame, 0], recv_sem=rim_recv.at[frame, 0],
            device_id=((me + N - 1) % N, side), device_id_type=MESH,
        )
        down = pltpu.make_async_remote_copy(
            src_ref=video.at[frame, R - 1], dst_ref=rows.at[frame, 0],
            send_sem=rim_send.at[frame, 1], recv_sem=rim_recv.at[frame, 1],
            device_id=((me + 1) % N, side), device_id_type=MESH,
        )
        return up, down

    def wait_rims(frame):
        for copy in rim_copies(frame):
            copy.wait()

        @pl.when(me == 0)
        def _():
            rows[frame, 0] = jnp.zeros((W, C), BF16)

        @pl.when(me == N - 1)
        def _():
            rows[frame, R + 1] = jnp.zeros((W, C), BF16)

    column = lax.broadcasted_iota(jnp.int32, (W, C), 0)

    def shift(frame, i):
        row = rows[frame, i].astype(F32)
        left[i] = jnp.where(column == 0, 0.0, pltpu.roll(row, 1, 0)).astype(BF16)
        right[i] = jnp.where(column == W - 1, 0.0, pltpu.roll(row, W - 1, 0)).astype(BF16)

    def convolve(frame, pair):
        first = 2 * pair
        pieces = (
            [left[first + j] for j in range(4)]
            + [rows[frame, first + j] for j in range(4)]
            + [right[first + j] for j in range(4)]
        )
        total = jnp.dot(jnp.concatenate(pieces, axis=1), weights[...], preferred_element_type=F32)
        upper = (total[:, :C] + bias[...]).reshape(N, COLS, C)
        lower = (total[:, C:] + bias[...]).reshape(N, COLS, C)
        both = jnp.concatenate([upper, lower], axis=1).astype(BF16)
        outgoing[frame, :, pl.ds(pl.multiple_of(pair * 2 * COLS, 2 * COLS), 2 * COLS), :] = both

    def inner(frame):
        load(frame).wait()
        pl.loop(1, R + 1)(lambda i: shift(frame, i))
        pl.loop(1, R // 2 - 1)(lambda pair: convolve(frame, pair))

    def outer(frame):
        wait_rims(frame)
        pl.loop(0, 2)(lambda k: shift(frame, k * (R + 1)))
        pl.loop(0, 2)(lambda k: convolve(frame, k * (R // 2 - 1)))

    def own(frame):
        return pltpu.make_async_copy(outgoing.at[frame, me], received.at[frame, me], own_sem.at[frame])

    def send(frame, slot, peer, where, start=0, size=BLOCK):
        part = pl.ds(start, size)
        pltpu.make_async_remote_copy(
            src_ref=outgoing.at[frame, peer, part], dst_ref=received.at[slot, me, part],
            send_sem=send_sem.at[slot], recv_sem=recv_sem.at[slot],
            device_id=(peer, where), device_id_type=MESH,
        ).start()

    head = frame_at(0)
    inner(head)
    pl.semaphore_wait(barrier, 2 * N - 1)
    for copy in rim_copies(head):
        copy.start()

    @pl.loop(1, N)
    def _(index):
        send(head, head, partner(me, index), side, EDGE, BLOCK - 2 * EDGE)

    for step in range(1, F):
        for copy in rim_copies(frame_at(step)):
            copy.start()
    outer(head)
    send(head, F, me, 1 - side)

    @pl.loop(1, N)
    def _(index):
        peer = partner(me, index)
        send(head, F, peer, 1 - side)
        send(head, head, peer, side, 0, EDGE)
        send(head, head, peer, side, BLOCK - EDGE, EDGE)

    own(head).start()

    @pl.loop(1, F)
    def _(step):
        frame = frame_at(step)
        inner(frame)
        outer(frame)

        def in_order(early):
            @pl.loop(1, N)
            def _(index):
                peer = partner(me, index)
                near = ((peer // 2) % 4 == 0) | ((peer // 2) % 4 == 3)

                @pl.when(((step < F - 1) | near) if early else ((step == F - 1) & jnp.logical_not(near)))
                def _():
                    send(frame, frame, peer, side)

        in_order(True)
        in_order(False)
        own(frame).start()

    def whole(slot, count, sem):
        part = received.at[slot, pl.ds(0, count)]
        return pltpu.make_async_copy(part, part, sem.at[slot])

    whole(F, N, recv_sem).wait()
    for step in range(F - 1):
        whole(frame_at(step), N - 1, recv_sem).wait()
        own(frame_at(step)).wait()

    slots = [1 + 3 * side, 2 - 2 * side, 3 - 2 * side, 4 - 2 * side]

    @pl.loop(0, N // GROUP)
    def _(index):
        blocks = pl.ds(pl.multiple_of(index * GROUP, GROUP), GROUP)
        out = pl.ds(pl.multiple_of(index * TILE, TILE), TILE)
        seen = [received[slot, blocks].reshape(TILE, C) for slot in slots]
        half = jnp.asarray(0.5, BF16)
        middles = [(seen[k] + seen[k + 1]) * half for k in range(3)]
        for k in range(2):
            even, odd = two_frames(
                middles[k], seen[k + 1], middles[k + 1], seen[k + 2], time_weights, time_bias[...]
            )
            early[2 * k, out] = even
            early[2 * k + 1, out] = odd

    last = frame_at(F - 1)
    for slot in range(F):
        whole(slot, N - 1, send_sem).wait()
    whole(F, N, send_sem).wait()
    whole(last, N - 1, recv_sem).wait()
    own(last).wait()


def exchange(video, spatial_taps, spatial_bias, temporal_taps, temporal_bias):
    return pl.pallas_call(
        exchange_body,
        out_shape=(
            pltpu.VMEM((F + 1, N, BLOCK, C), BF16),
            pltpu.VMEM((F, COUNT, C), BF16),
        ),
        in_specs=[pl.BlockSpec(memory_space=pltpu.HBM)] * 5,
        out_specs=[pl.BlockSpec(memory_space=pltpu.VMEM)] * 2,
        scratch_shapes=[
            pltpu.VMEM((F, R + 2, W, C), BF16),
            pltpu.VMEM((R + 2, W, C), BF16),
            pltpu.VMEM((R + 2, W, C), BF16),
            pltpu.VMEM((F, N, BLOCK, C), BF16),
            pltpu.VMEM((12 * C, 2 * C), BF16),
            pltpu.VMEM((4 * C, 2 * C), BF16),
            pltpu.VMEM((3, 3, C, C), BF16),
            pltpu.VMEM((3, C, C), BF16),
            pltpu.VMEM((1, C), F32),
            pltpu.VMEM((1, C), F32),
            pltpu.SemaphoreType.DMA((F,)),
            pltpu.SemaphoreType.DMA((4,)),
            pltpu.SemaphoreType.DMA((F, 2)),
            pltpu.SemaphoreType.DMA((F, 2)),
            pltpu.SemaphoreType.DMA((F + 1,)),
            pltpu.SemaphoreType.DMA((F + 1,)),
            pltpu.SemaphoreType.DMA((F,)),
        ],
        compiler_params=pltpu.CompilerParams(
            collective_id=0, has_side_effects=True, vmem_limit_bytes=30 * 2**20
        ),
        cost_estimate=pl.CostEstimate(
            flops=2 * 9 * C * C * F * R * W + 3 * C * C * 2 * F * COUNT,
            bytes_accessed=F * R * W * C * 2,
            transcendentals=0,
        ),
        name="spatial_exchange",
    )(
        *(
            pltpu.with_memory_space_constraint(operand, pltpu.HBM)
            for operand in (video, spatial_taps, spatial_bias, temporal_taps, temporal_bias)
        )
    )


def late_body(received, early, taps, bias, doubled, weights, late, early_sem, late_sem):
    side = lax.axis_index("frames")
    copies = [
        pltpu.make_async_copy(early.at[k], doubled.at[F * (1 - side) + k], early_sem.at[k]) for k in range(F)
    ]
    for copy in copies:
        copy.start()
    spread_taps(taps, weights)
    zero, half = jnp.asarray(0.0, BF16), jnp.asarray(0.5, BF16)
    slots = [side, 2 * side, 1 + 2 * side, 2 + side]

    def store(index):
        out = pl.ds(pl.multiple_of(index * TILE, TILE), TILE)
        return pltpu.make_async_copy(
            late.at[:, out], doubled.at[pl.ds(F * side, F), out], late_sem.at[index]
        )

    @pl.loop(0, N // GROUP)
    def _(index):
        blocks = pl.ds(pl.multiple_of(index * GROUP, GROUP), GROUP)
        out = pl.ds(pl.multiple_of(index * TILE, TILE), TILE)
        seen = [received[slot, blocks].reshape(TILE, C) for slot in slots]
        middles = [(seen[k] + seen[k + 1]) * half for k in range(3)]
        middles[0] = jnp.where(side == 0, zero, middles[0])
        middles[2] = jnp.where(side == 0, middles[2], seen[2])
        seen[3] = jnp.where(side == 0, seen[3], zero)
        for k in range(2):
            even, odd = two_frames(
                middles[k], seen[k + 1], middles[k + 1], seen[k + 2], weights, bias[...]
            )
            late[2 * k, out] = even
            late[2 * k + 1, out] = odd
        store(index).start()

    pl.loop(0, N // GROUP)(lambda index: store(index).wait())
    for copy in copies:
        copy.wait()


def finish(received, early, taps, bias):
    return pl.pallas_call(
        late_body,
        out_shape=jax.ShapeDtypeStruct((2 * F, COUNT, C), BF16),
        in_specs=[pl.BlockSpec(memory_space=pltpu.VMEM)] * 4,
        out_specs=pl.BlockSpec(memory_space=pl.ANY),
        scratch_shapes=[
            pltpu.VMEM((4 * C, 2 * C), BF16),
            pltpu.VMEM((F, COUNT, C), BF16),
            pltpu.SemaphoreType.DMA((F,)),
            pltpu.SemaphoreType.DMA((N // GROUP,)),
        ],
        compiler_params=pltpu.CompilerParams(vmem_limit_bytes=16 * 2**20),
        cost_estimate=pl.CostEstimate(
            flops=3 * C * C * 2 * F * COUNT, bytes_accessed=8 * COUNT * C * 2, transcendentals=0
        ),
        name="late_frames",
    )(
        pltpu.with_memory_space_constraint(received, pltpu.VMEM),
        pltpu.with_memory_space_constraint(early, pltpu.VMEM),
        taps,
        bias,
    )


def per_device(video, spatial_kernel, spatial_bias, temporal_kernel, temporal_bias):
    time_bias = temporal_bias.reshape(1, C)
    received, early = exchange(
        video, spatial_kernel, spatial_bias.reshape(1, C), temporal_kernel, time_bias
    )
    doubled = finish(received, early, temporal_kernel, time_bias)
    return doubled.reshape(2 * F, N * R, COLS, C)


def solution(mesh):
    placed = (P("frames", "rows", None, None), P(), P(), P(), P())
    return jax.shard_map(
        per_device,
        mesh=mesh,
        in_specs=placed,
        out_specs=P("frames", None, "rows", None),
        check_vma=False,
    )
```

```python
import jax
import jax.numpy as jnp
from jax import lax
from jax.experimental import pallas as pl
from jax.experimental.pallas import tpu as pltpu
from jax.sharding import PartitionSpec as P

MESH = pl.DeviceIdType.MESH
C = 128
F = 4
R = 12
W = 512
N = 64
COLS = W // N
BLOCK = R * COLS
EDGE = 2 * COLS
COUNT = N * BLOCK
GROUP = 8
TILE = GROUP * BLOCK
BF16 = jnp.bfloat16
F32 = jnp.float32


def partner(row, step):
    mixed = (21 * step + 6 * step * step) % N
    y = (row // 16 + (mixed // 4)) % 4
    z = (row // 8 + mixed // 16) % 2
    x = (row // 2 + (mixed)) % 4
    core = (row + mixed // 32) % 2
    return ((y * 2 + z) * 4 + x) * 2 + core


def spread_taps(taps, weights):
    for j in range(4):
        for o in range(2):
            d = j - o
            block = taps[d] if 0 <= d < 3 else jnp.zeros((C, C), BF16)
            weights[pl.ds(j * C, C), pl.ds(o * C, C)] = block


def two_frames(before, frame, middle, following, weights, bias):
    window = jnp.concatenate([before, frame, middle, following], axis=1)
    total = jnp.dot(window, weights[...], preferred_element_type=F32)
    even = total[:, :C] + (frame.astype(F32) + bias)
    odd = total[:, C:] + (middle.astype(F32) + bias)
    return even.astype(BF16), odd.astype(BF16)


def exchange_body(
    video, spatial_taps, spatial_bias, temporal_taps, temporal_bias,
    received, early,
    rows, left, right, outgoing, weights, time_weights, taps, time_taps, bias, time_bias,
    load_sem, small_sem, rim_send, rim_recv, send_sem, recv_sem, own_sem,
):
    me = lax.axis_index("rows")
    side = lax.axis_index("frames")
    barrier = pltpu.get_barrier_semaphore()

    def frame_at(step):
        return step * (2 * side - 1) + (F - 1) * (1 - side)

    def load(frame):
        return pltpu.make_async_copy(video.at[frame], rows.at[frame, pl.ds(1, R)], load_sem.at[frame])

    load(frame_at(0)).start()
    small = [
        pltpu.make_async_copy(source, target, small_sem.at[k])
        for k, (source, target) in enumerate(
            [(spatial_taps, taps), (spatial_bias, bias), (temporal_taps, time_taps), (temporal_bias, time_bias)]
        )
    ]
    for copy in small:
        copy.start()

    @pl.loop(1, N, unroll=63)
    def _(step):
        peer = me + step - N * ((me + step) // N)
        pl.semaphore_signal(barrier, inc=1, device_id=(peer, side), device_id_type=MESH)
        pl.semaphore_signal(barrier, inc=1, device_id=(peer, 1 - side), device_id_type=MESH)

    pl.semaphore_signal(barrier, inc=1, device_id=(me, 1 - side), device_id_type=MESH)

    for step in range(1, F):
        load(frame_at(step)).start()
    for copy in small:
        copy.wait()
    for b in range(3):
        for j in range(4):
            for o in range(2):
                a = j - o
                block = taps[a, b] if 0 <= a < 3 else jnp.zeros((C, C), BF16)
                weights[pl.ds((b * 4 + j) * C, C), pl.ds(o * C, C)] = block
    spread_taps(time_taps, time_weights)

    def rim_copies(frame):
        up = pltpu.make_async_remote_copy(
            src_ref=video.at[frame, 0], dst_ref=rows.at[frame, R + 1],
            send_sem=rim_send.at[frame, 0], recv_sem=rim_recv.at[frame, 0],
            device_id=((me + N - 1) % N, side), device_id_type=MESH,
        )
        down = pltpu.make_async_remote_copy(
            src_ref=video.at[frame, R - 1], dst_ref=rows.at[frame, 0],
            send_sem=rim_send.at[frame, 1], recv_sem=rim_recv.at[frame, 1],
            device_id=((me + 1) % N, side), device_id_type=MESH,
        )
        return up, down

    def wait_rims(frame):
        for copy in rim_copies(frame):
            copy.wait()

        @pl.when(me == 0)
        def _():
            rows[frame, 0] = jnp.zeros((W, C), BF16)

        @pl.when(me == N - 1)
        def _():
            rows[frame, R + 1] = jnp.zeros((W, C), BF16)

    column = lax.broadcasted_iota(jnp.int32, (W, C), 0)

    def shift(frame, i):
        row = rows[frame, i].astype(F32)
        left[i] = jnp.where(column == 0, 0.0, pltpu.roll(row, 1, 0)).astype(BF16)
        right[i] = jnp.where(column == W - 1, 0.0, pltpu.roll(row, W - 1, 0)).astype(BF16)

    def convolve(frame, pair):
        first = 2 * pair
        pieces = (
            [left[first + j] for j in range(4)]
            + [rows[frame, first + j] for j in range(4)]
            + [right[first + j] for j in range(4)]
        )
        total = jnp.dot(jnp.concatenate(pieces, axis=1), weights[...], preferred_element_type=F32)
        upper = (total[:, :C] + bias[...]).reshape(N, COLS, C)
        lower = (total[:, C:] + bias[...]).reshape(N, COLS, C)
        both = jnp.concatenate([upper, lower], axis=1).astype(BF16)
        outgoing[frame, :, pl.ds(pl.multiple_of(pair * 2 * COLS, 2 * COLS), 2 * COLS), :] = both

    def inner(frame):
        load(frame).wait()
        pl.loop(1, R + 1)(lambda i: shift(frame, i))
        pl.loop(1, R // 2 - 1)(lambda pair: convolve(frame, pair))

    def outer(frame):
        wait_rims(frame)
        pl.loop(0, 2)(lambda k: shift(frame, k * (R + 1)))
        pl.loop(0, 2)(lambda k: convolve(frame, k * (R // 2 - 1)))

    def own(frame):
        return pltpu.make_async_copy(outgoing.at[frame, me], received.at[frame, me], own_sem.at[frame])

    def send(frame, slot, peer, where, start=0, size=BLOCK):
        part = pl.ds(start, size)
        pltpu.make_async_remote_copy(
            src_ref=outgoing.at[frame, peer, part], dst_ref=received.at[slot, me, part],
            send_sem=send_sem.at[slot], recv_sem=recv_sem.at[slot],
            device_id=(peer, where), device_id_type=MESH,
        ).start()

    head = frame_at(0)
    inner(head)
    pl.semaphore_wait(barrier, 2 * N - 1)
    for copy in rim_copies(head):
        copy.start()

    @pl.loop(1, N)
    def _(index):
        send(head, head, partner(me, index), side, EDGE, BLOCK - 2 * EDGE)

    for step in range(1, F):
        for copy in rim_copies(frame_at(step)):
            copy.start()
    outer(head)
    send(head, F, me, 1 - side)

    @pl.loop(1, N)
    def _(index):
        peer = partner(me, index)
        send(head, F, peer, 1 - side)
        send(head, head, peer, side, 0, EDGE)
        send(head, head, peer, side, BLOCK - EDGE, EDGE)

    own(head).start()

    @pl.loop(1, F)
    def _(step):
        frame = frame_at(step)
        inner(frame)
        outer(frame)

        def in_order(early):
            @pl.loop(1, N)
            def _(index):
                peer = partner(me, index)
                near = ((peer // 2) % 4 == 0) | ((peer // 2) % 4 == 3)

                @pl.when(((step < F - 1) | near) if early else ((step == F - 1) & jnp.logical_not(near)))
                def _():
                    send(frame, frame, peer, side)

        in_order(True)
        in_order(False)
        own(frame).start()

    def whole(slot, count, sem):
        part = received.at[slot, pl.ds(0, count)]
        return pltpu.make_async_copy(part, part, sem.at[slot])

    whole(F, N, recv_sem).wait()
    for step in range(F - 1):
        whole(frame_at(step), N - 1, recv_sem).wait()
        own(frame_at(step)).wait()

    slots = [1 + 3 * side, 2 - 2 * side, 3 - 2 * side, 4 - 2 * side]

    @pl.loop(0, N // GROUP)
    def _(index):
        blocks = pl.ds(pl.multiple_of(index * GROUP, GROUP), GROUP)
        out = pl.ds(pl.multiple_of(index * TILE, TILE), TILE)
        seen = [received[slot, blocks].reshape(TILE, C) for slot in slots]
        half = jnp.asarray(0.5, BF16)
        middles = [(seen[k] + seen[k + 1]) * half for k in range(3)]
        for k in range(2):
            even, odd = two_frames(
                middles[k], seen[k + 1], middles[k + 1], seen[k + 2], time_weights, time_bias[...]
            )
            early[2 * k, out] = even
            early[2 * k + 1, out] = odd

    last = frame_at(F - 1)
    for slot in range(F):
        whole(slot, N - 1, send_sem).wait()
    whole(F, N, send_sem).wait()
    whole(last, N - 1, recv_sem).wait()
    own(last).wait()


def exchange(video, spatial_taps, spatial_bias, temporal_taps, temporal_bias):
    return pl.pallas_call(
        exchange_body,
        out_shape=(
            pltpu.VMEM((F + 1, N, BLOCK, C), BF16),
            pltpu.VMEM((F, COUNT, C), BF16),
        ),
        in_specs=[pl.BlockSpec(memory_space=pltpu.HBM)] * 5,
        out_specs=[pl.BlockSpec(memory_space=pltpu.VMEM)] * 2,
        scratch_shapes=[
            pltpu.VMEM((F, R + 2, W, C), BF16),
            pltpu.VMEM((R + 2, W, C), BF16),
            pltpu.VMEM((R + 2, W, C), BF16),
            pltpu.VMEM((F, N, BLOCK, C), BF16),
            pltpu.VMEM((12 * C, 2 * C), BF16),
            pltpu.VMEM((4 * C, 2 * C), BF16),
            pltpu.VMEM((3, 3, C, C), BF16),
            pltpu.VMEM((3, C, C), BF16),
            pltpu.VMEM((1, C), F32),
            pltpu.VMEM((1, C), F32),
            pltpu.SemaphoreType.DMA((F,)),
            pltpu.SemaphoreType.DMA((4,)),
            pltpu.SemaphoreType.DMA((F, 2)),
            pltpu.SemaphoreType.DMA((F, 2)),
            pltpu.SemaphoreType.DMA((F + 1,)),
            pltpu.SemaphoreType.DMA((F + 1,)),
            pltpu.SemaphoreType.DMA((F,)),
        ],
        compiler_params=pltpu.CompilerParams(
            collective_id=0, has_side_effects=True, vmem_limit_bytes=30 * 2**20
        ),
        cost_estimate=pl.CostEstimate(
            flops=2 * 9 * C * C * F * R * W + 3 * C * C * 2 * F * COUNT,
            bytes_accessed=F * R * W * C * 2,
            transcendentals=0,
        ),
        name="spatial_exchange",
    )(
        *(
            pltpu.with_memory_space_constraint(operand, pltpu.HBM)
            for operand in (video, spatial_taps, spatial_bias, temporal_taps, temporal_bias)
        )
    )


def late_body(received, early, taps, bias, doubled, weights, late, early_sem, late_sem):
    side = lax.axis_index("frames")
    copies = [
        pltpu.make_async_copy(early.at[k], doubled.at[F * (1 - side) + k], early_sem.at[k]) for k in range(F)
    ]
    for copy in copies:
        copy.start()
    spread_taps(taps, weights)
    zero, half = jnp.asarray(0.0, BF16), jnp.asarray(0.5, BF16)
    slots = [side, 2 * side, 1 + 2 * side, 2 + side]

    def store(index):
        out = pl.ds(pl.multiple_of(index * TILE, TILE), TILE)
        return pltpu.make_async_copy(
            late.at[:, out], doubled.at[pl.ds(F * side, F), out], late_sem.at[index]
        )

    @pl.loop(0, N // GROUP)
    def _(index):
        blocks = pl.ds(pl.multiple_of(index * GROUP, GROUP), GROUP)
        out = pl.ds(pl.multiple_of(index * TILE, TILE), TILE)
        seen = [received[slot, blocks].reshape(TILE, C) for slot in slots]
        middles = [(seen[k] + seen[k + 1]) * half for k in range(3)]
        middles[0] = jnp.where(side == 0, zero, middles[0])
        middles[2] = jnp.where(side == 0, middles[2], seen[2])
        seen[3] = jnp.where(side == 0, seen[3], zero)
        for k in range(2):
            even, odd = two_frames(
                middles[k], seen[k + 1], middles[k + 1], seen[k + 2], weights, bias[...]
            )
            late[2 * k, out] = even
            late[2 * k + 1, out] = odd
        store(index).start()

    pl.loop(0, N // GROUP)(lambda index: store(index).wait())
    for copy in copies:
        copy.wait()


def finish(received, early, taps, bias):
    return pl.pallas_call(
        late_body,
        out_shape=jax.ShapeDtypeStruct((2 * F, COUNT, C), BF16),
        in_specs=[pl.BlockSpec(memory_space=pltpu.VMEM)] * 4,
        out_specs=pl.BlockSpec(memory_space=pl.ANY),
        scratch_shapes=[
            pltpu.VMEM((4 * C, 2 * C), BF16),
            pltpu.VMEM((F, COUNT, C), BF16),
            pltpu.SemaphoreType.DMA((F,)),
            pltpu.SemaphoreType.DMA((N // GROUP,)),
        ],
        compiler_params=pltpu.CompilerParams(vmem_limit_bytes=16 * 2**20),
        cost_estimate=pl.CostEstimate(
            flops=3 * C * C * 2 * F * COUNT, bytes_accessed=8 * COUNT * C * 2, transcendentals=0
        ),
        name="late_frames",
    )(
        pltpu.with_memory_space_constraint(received, pltpu.VMEM),
        pltpu.with_memory_space_constraint(early, pltpu.VMEM),
        taps,
        bias,
    )


def per_device(video, spatial_kernel, spatial_bias, temporal_kernel, temporal_bias):
    time_bias = temporal_bias.reshape(1, C)
    received, early = exchange(
        video, spatial_kernel, spatial_bias.reshape(1, C), temporal_kernel, time_bias
    )
    doubled = finish(received, early, temporal_kernel, time_bias)
    return doubled.reshape(2 * F, N * R, COLS, C)


def solution(mesh):
    placed = (P("frames", "rows", None, None), P(), P(), P(), P())
    return jax.shard_map(
        per_device,
        mesh=mesh,
        in_specs=placed,
        out_specs=P("frames", None, "rows", None),
        check_vma=False,
    )
```
